256 devices in a mesh: band: 64 (over y, z, core), grp: 4 (over x).
Axes of the slice: x: 4, y: 4, z: 8, core: 2. Of those that a mesh axis runs over, the one named last changes fastest.
Arguments:
- coarse: bfloat16 [64, 60, 73, 384], P('band', 'grp'), may hold values from -6 to 6
- region_lat: int32 [12], replicated, may hold values from 0 to 62
- region_lon: int32 [12], replicated, may hold values from 0 to 59
- region_order: int32 [12], replicated, may hold values from 0 to 11, each once
- conv_weight: bfloat16 [9, 128, 73], replicated, may hold values from -0.25 to 0.25
- conv_bias: float32 [128], replicated, may hold values from -3 to 3
Outputs:
- tiles: bfloat16 [12, 64, 128, 3136], P('grp', 'band')
The draws below stay inside these ranges and needn't reach their ends.
All inputs are finite; a program needn't handle non-finite values.
Results may differ from the reference program's by a relative error of at most 0.0042.
Values may be sent and summed in bfloat16 or wider, within the bound.
No kernel may reach another device: no remote copies, remote signals or barrier semaphores. Data moves between devices by JAX's collectives and lax.ppermute only.
A program may use at most 64 MiB of HBM per device.

```python
import math
import jax
import jax.numpy as jnp
import numpy as np
from jax import lax

CH = 73
CO = 128
FN = 448
BR = 16
BC = 24
LONB = 60
TCOLS = 8
REGIONS = 12
LATB = 64
TROWS = 8
TH = 56
TW = 56


def plant(entries, own_key, smallest, high):
    dims = entries.shape
    place = [jax.random.randint(jax.random.fold_in(own_key, axis), (), 0, dims[axis]) for axis in range(len(dims))]
    entries = entries.at[tuple(place)].set(smallest)
    longest = dims.index(max(dims))
    place[longest] = (place[longest] + 1) % dims[longest]
    return entries.at[tuple(place)].set(high)


def levels(own_key, shape, shards, low, high):
    gain, own = 1.0, jax.random.fold_in(own_key, 6)
    for dim, parts in shards:
        heights = jnp.exp(jax.random.uniform(jax.random.fold_in(own, dim), (parts,), jnp.float32, low / len(shards), high / len(shards)))
        gain = gain * jnp.repeat(heights, shape[dim] // parts).reshape([-1 if axis == dim else 1 for axis in range(len(shape))])
    return gain


def rank_bounds(number_of, lean):
    portions = [(1 << 20) // math.isqrt(grade ** lean) + 1 for grade in range(1, number_of + 1)]
    width = 1 + sum(portions) // (1 << 30)
    return np.cumsum(np.array([max(1, weight // width) for weight in portions]))


def ranked(rng, dims, number_of, lean):
    table = rank_bounds(number_of, lean)
    lot = jax.random.randint(jax.random.fold_in(rng, 1), dims, 0, int(table[number_of - 1]))
    rank = jnp.searchsorted(jnp.asarray(table, jnp.int32), lot, side="right")
    return jax.random.permutation(jax.random.fold_in(rng, 2), number_of)[rank].astype(jnp.int32)


def gaussian(own_key, dims, deviation, most, cuts=(), kind=jnp.bfloat16):
    values = deviation * jax.random.normal(own_key, dims, jnp.float32)
    if cuts:
        values = values * levels(own_key, dims, cuts, -0.22, 0.18)
    return jnp.clip(values, -most, most).astype(kind)


def setup_inputs(seed: int = 0) -> dict:
    key_list = jax.random.split(jax.random.key(seed), 7)
    return {
        "coarse": gaussian(key_list[0], (LATB, LONB, CH, BR * BC), 1.0, 6.0, ((0, 64), (1, 4))),
        "region_lat": plant(ranked(key_list[1], (REGIONS,), LATB - 1, 2), jax.random.fold_in(key_list[1], 3), 0, (LATB - 1) - 1).astype(jnp.int32),
        "region_lon": plant(jax.random.randint(key_list[2], (REGIONS,), 0, LONB), jax.random.fold_in(key_list[2], 1), 0, LONB - 1).astype(jnp.int32),
        "region_order": jax.random.permutation(key_list[3], REGIONS).astype(jnp.int32),
        "conv_weight": gaussian(key_list[4], (9, CO, CH), (9 * CH) ** -0.5, 0.25),
        "conv_bias": gaussian(key_list[5], (CO,), 0.5, 3.0, (), jnp.float32),
    }


def bilinear(positions, node_count, fine_count):
    coords = (positions.astype(jnp.float32) + 0.5) * (node_count / fine_count) - 0.5
    coords = jnp.clip(coords, 0.0, node_count - 1.0)
    centres = jnp.arange(node_count, dtype=jnp.float32)
    weight = jnp.maximum(0.0, 1.0 - jnp.abs(coords[:, None] - centres[None, :]))
    inside = (positions >= 0) & (positions < fine_count)
    return jnp.where(inside[:, None], weight, 0.0)


def as_field(blocks):
    count_slots, channels = blocks.shape[0], blocks.shape[3]
    shaped = blocks.reshape(count_slots, 2, 2, channels, BR, BC)
    return shaped.transpose(0, 3, 1, 4, 2, 5).reshape(count_slots, channels, 2 * BR, 2 * BC)


def upsample(window, row_weights, col_weights):
    half_done = jnp.einsum("pr,scrw->scpw", row_weights, window, precision=lax.Precision.HIGHEST)
    return jnp.einsum("scpw,qw->scpq", half_done, col_weights, precision=lax.Precision.HIGHEST).astype(jnp.bfloat16)


def convolve_exact(padded, conv_weight, conv_bias, tile_height, tile_width):
    channels = padded.shape[0]
    summed = jnp.zeros((conv_weight.shape[1], tile_height * tile_width), jnp.float32)
    for tap_index in range(9):
        row_step, col_step = divmod(tap_index, 3)
        patch_view = padded[:, row_step:row_step + tile_height, col_step:col_step + tile_width]
        patch_view = patch_view.reshape(channels, tile_height * tile_width)
        summed = summed + jnp.einsum("oc,cn->on", conv_weight[tap_index], patch_view, precision=lax.Precision.HIGHEST)
    return jax.nn.silu(summed + conv_bias[:, None]).astype(jnp.bfloat16)


def reference(coarse, region_lat, region_lon, region_order, conv_weight, conv_bias):
    positions = jnp.arange(-1, FN + 1, dtype=jnp.int32)
    row_weights = bilinear(positions, 2 * BR, FN)
    col_weights = bilinear(positions, 2 * BC, FN)
    offsets = jnp.arange(2, dtype=jnp.int32)
    weight_exact = conv_weight.astype(jnp.float32)

    def per_region(region):
        lat_ids = region_lat[region] + offsets
        lon_ids = (region_lon[region] + offsets) % LONB
        blocks = coarse[lat_ids[:, None], lon_ids[None, :]]
        window = as_field(blocks[None]).astype(jnp.float32)
        padded = upsample(window, row_weights, col_weights)[0].astype(jnp.float32)
        result = convolve_exact(padded, weight_exact, conv_bias, FN, FN)
        result = result.reshape(CO, TROWS, TH, TCOLS, TW).transpose(1, 3, 0, 2, 4)
        return result.reshape(TROWS * TCOLS, CO, TH * TW)

    return lax.map(per_region, region_order)
```

```python
import functools

import jax
import jax.numpy as jnp
from jax import lax
from jax.experimental import pallas as pl
from jax.experimental.pallas import tpu as pltpu
from jax.sharding import PartitionSpec as P

CH = 73
CO = 128
FN = 448
BR = 16
BC = 24
CELLS = BR * BC
TCOLS = 8
TH = 56
TW = 56
WR = 6
WC = 8
MAIN = 64
REST = CH - MAIN
ROW = 64
UROWS = 8
CAPACITIES = (1, 2, 3, 4, 12)
F32 = jnp.float32
BF16 = jnp.bfloat16


def bilinear(positions, node_count, fine_count, nodes):
    coords = (positions.astype(F32) + 0.5) * (node_count / fine_count) - 0.5
    coords = jnp.clip(coords, 0.0, node_count - 1.0)
    weight = jnp.maximum(0.0, 1.0 - jnp.abs(coords - nodes.astype(F32)))
    inside = (positions >= 0) & (positions < fine_count)
    return jnp.where(inside, weight, 0.0)


def plan_kernel(lat, lon, order, table, chips, places, branch, counts):
    band, group = lax.axis_index("band"), lax.axis_index("grp")
    chip, core = band // 2, lax.rem(band, 2)
    for n in range(48):
        table[n] = -1
    held = []
    for i in range(12):
        region = order[i]
        lat0, lon0 = lat[region], lon[region]
        lon1 = jnp.where(lon0 == 59, 0, lon0 + 1)
        m0, m1 = lax.shift_right_logical(lat0, 1), lax.shift_right_logical(lat0 + 1, 1)
        g0, g1 = [
            (x >= 15).astype(jnp.int32) + (x >= 30).astype(jnp.int32) + (x >= 45).astype(jnp.int32)
            for x in (lon0, lon1)
        ]
        for m in (m0, m1):
            for g in (g0, g1):
                counts[g * 32 + m] = 0
        held.append((lat0, lon0, lon1, m0, m1, g0, g1))
    counts[group * 32 + chip] = 0
    most = jnp.int32(0)
    for i, (lat0, lon0, lon1, m0, m1, g0, g1) in enumerate(held):
        here = (g0 == group) | (g1 == group)
        chips[2 * i] = m0
        chips[2 * i + 1] = m1
        at0, at1 = group * 32 + m0, group * 32 + m1
        places[2 * i] = jnp.where(here, counts[at0], -1)
        places[2 * i + 1] = jnp.where(here & (m0 != m1), counts[at1], -1)

        @pl.when(here & ((m0 == chip) | (m1 == chip)))
        def _():
            q = counts[group * 32 + chip]
            for j in range(2):
                row = lat0 + j - 2 * chip
                for k, at in enumerate((lon0, lon1)):
                    col = at - 15 * group
                    ok = (row >= 0) & (row < 2) & (col >= 0) & (col < 15)
                    side = jnp.where(row == core, 0, 16)
                    table[q * 4 + j * 2 + k] = jnp.where(ok, side + col, -1)

        new_m = (m0 != m1).astype(jnp.int32)
        new_g = (g0 != g1).astype(jnp.int32)
        for m, dm in ((m0, jnp.int32(1)), (m1, new_m)):
            for g, dg in ((g0, jnp.int32(1)), (g1, new_g)):
                n = counts[g * 32 + m] + dm * dg
                counts[g * 32 + m] = n
                most = jnp.maximum(most, n)
    step = jnp.int32(0)
    for cap in CAPACITIES[:-1]:
        step = step + (most > cap).astype(jnp.int32)
    branch[0] = step


def plan(lat, lon, order):
    smem = pl.BlockSpec(memory_space=pltpu.SMEM)
    return pl.pallas_call(
        plan_kernel,
        out_shape=[jax.ShapeDtypeStruct((n,), jnp.int32) for n in (48, 24, 24, 1)],
        in_specs=[smem] * 3,
        out_specs=[smem] * 4,
        scratch_shapes=[pltpu.SMEM((128,), jnp.int32)],
        name="plan",
    )(lat, lon, order)


def payload_rows(capacity):
    return 24 * capacity + 8 * ((capacity + 1) // 2)


def pick_kernel(capacity, table, own, other, out, window, blocks, sems):
    core = lax.rem(lax.axis_index("band"), 2)

    def copies(n):
        code = table[n]
        mine = pltpu.make_async_copy(own.at[code], blocks.at[n], sems.at[n])
        near = pltpu.make_async_copy(other.at[code - 16], blocks.at[n], sems.at[n])
        return code, mine, near

    for n in range(4 * capacity):
        code, mine, near = copies(n)

        @pl.when((code >= 0) & (code < 16))
        def _():
            mine.start()

        @pl.when(code >= 16)
        def _():
            near.start()

    lane = lax.broadcasted_iota(jnp.int32, (8, 128), 1)
    turn = (
        lax.broadcasted_iota(jnp.int32, (CELLS, CELLS), 0)
        == lax.broadcasted_iota(jnp.int32, (CELLS, CELLS), 1)
    ).astype(BF16)
    zeros = jnp.zeros((ROW, 128), F32)
    for q in range(capacity):
        base = q * 34 * ROW
        window[base : base + ROW] = zeros
        window[base + 33 * ROW : base + 34 * ROW] = zeros
        for r in range(1, 33):
            window[base + r * ROW : base + r * ROW + 8] = zeros[:8]
            window[base + r * ROW + 56 : base + r * ROW + 64] = zeros[:8]
        for j in range(2):
            for k in range(2):
                n = q * 4 + j * 2 + k
                code, mine, near = copies(n)

                @pl.when((code >= 0) & (code < 16))
                def _():
                    mine.wait()

                @pl.when(code >= 16)
                def _():
                    near.wait()

                block = blocks[n]
                block = jnp.where(code >= 0, block, jnp.zeros_like(block))
                turned = lax.dot_general(
                    turn, block, (((1,), (1,)), ((), ())), preferred_element_type=F32
                )
                for r in range(BR):
                    at = base + (16 * j + r + 1) * ROW + 8 + BC * k
                    window[at : at + BC, 0:CH] = turned[r * BC : (r + 1) * BC]

    def emit(a, carry):
        for b in range(4):
            mains, rests = [], []
            for q in range(capacity):
                rows = []
                for i in range(WR):
                    at = q * 34 * ROW + i * ROW + 7 + 12 * b + 6 * core + a * 4 * ROW
                    rows.append(window[pl.ds(at, WC)])
                for i in range(3):
                    mains.append(
                        jnp.where(lane < MAIN, rows[i], pltpu.roll(rows[i + 3], MAIN, 1))
                    )
                side = 64 * (q % 2)
                rest = jnp.zeros((8, 128), F32)
                for i in range(WR):
                    lo = side + REST * i
                    moved = pltpu.roll(rows[i], (lo - MAIN) % 128, 1)
                    rest = jnp.where((lane >= lo) & (lane < lo + REST), moved, rest)
                if q % 2 == 0:
                    rests.append(rest)
                else:
                    rests[-1] = rests[-1] + rest
            out[4 * a + b] = jnp.concatenate(mains + rests, axis=0).astype(BF16)
        return carry

    lax.fori_loop(0, 8, emit, 0)


def pick(capacity, table, own, other):
    vmem = pl.BlockSpec(memory_space=pltpu.VMEM)
    smem = pl.BlockSpec(memory_space=pltpu.SMEM)
    hbm = pl.BlockSpec(memory_space=pl.ANY)
    return pl.pallas_call(
        functools.partial(pick_kernel, capacity),
        out_shape=jax.ShapeDtypeStruct((32, payload_rows(capacity), 128), BF16),
        in_specs=[smem, hbm, hbm],
        out_specs=vmem,
        scratch_shapes=[
            pltpu.VMEM((capacity * 34 * ROW, 128), F32),
            pltpu.VMEM((4 * capacity, CH, CELLS), BF16),
            pltpu.SemaphoreType.DMA((4 * capacity,)),
        ],
        compiler_params=pltpu.CompilerParams(vmem_limit_bytes=40 * 2**20),
        name="pick",
    )(table, own, other)


def regroup_kernel(capacity, chips, places, got, out):
    lane = lax.broadcasted_iota(jnp.int32, (8, 128), 1)
    def gather(slot, carry):
        main = jnp.zeros((24, 128), F32)
        rest = jnp.zeros((8, 128), F32)
        for j in range(2):
            place = places[slot * 2 + j]
            part = got[chips[slot * 2 + j]].astype(F32)
            for q in range(capacity):
                here = place == q
                main = main + jnp.where(here, part[24 * q : 24 * q + 24], 0.0)
                at = 24 * capacity + 8 * (q // 2)
                side = part[at : at + 8]
                if q % 2:
                    side = pltpu.roll(side, 64, 1)
                rest = rest + jnp.where(here, side, 0.0)
        rows = []
        for i in range(WR):
            body = main[8 * (i % 3) : 8 * (i % 3) + 8]
            if i >= 3:
                body = pltpu.roll(body, 64, 1)
            tail = pltpu.roll(rest, (MAIN - REST * i) % 128, 1)
            row = jnp.where(lane < MAIN, body, jnp.where(lane < CH, tail, 0.0))
            rows.append(row)
        out[slot] = jnp.concatenate(rows, axis=0).astype(BF16)
        return carry

    lax.fori_loop(0, 12, gather, 0, unroll=capacity <= 2)


def regroup(capacity, chips, places, got):
    vmem = pl.BlockSpec(memory_space=pltpu.VMEM)
    smem = pl.BlockSpec(memory_space=pltpu.SMEM)
    return pl.pallas_call(
        functools.partial(regroup_kernel, capacity),
        out_shape=jax.ShapeDtypeStruct((12, WR * WC, 128), BF16),
        in_specs=[smem, smem, vmem],
        out_specs=vmem,
        compiler_params=pltpu.CompilerParams(vmem_limit_bytes=24 * 2**20),
        name="regroup",
    )(chips, places, got)


def conv_kernel(win, weight, bias, row_part, col_part, out, taps_hi):
    @pl.when(pl.program_id(0) == 0)
    def _():
        cells = win[0].astype(F32)
        for g in range(1, 4):
            cells = cells + win[g].astype(F32)
        cells = cells.astype(BF16)[:, :CH]
        taps = lax.dot_general(
            cells, weight[...], (((1,), (1,)), ((), ())), preferred_element_type=F32
        )
        taps = (taps * 0.5).astype(BF16)
        n = WR * WC
        for t in range(9):
            for s in range(3):
                taps_hi[t * n : (t + 1) * n, s * CO : (s + 1) * CO] = taps[
                    s * n : (s + 1) * n, t * CO : (t + 1) * CO
                ]

    cols = col_part[...]
    rows = row_part[...]
    spread = jnp.concatenate(
        [(cols * rows[u : u + 1]).astype(BF16) for u in range(UROWS)], axis=0
    )
    half = jnp.dot(spread, taps_hi[...], preferred_element_type=F32)
    for s in range(3):
        h = half[:, s * CO : (s + 1) * CO] + 0.5 * bias[...]
        out[s, 0] = (h + h * jnp.tanh(h)).astype(BF16)


def convolve(win, weight, bias, row_part, col_part):
    depth = 9 * WR * WC
    return pl.pallas_call(
        conv_kernel,
        grid=(TH // UROWS,),
        out_shape=jax.ShapeDtypeStruct((3, 1, TH * TW, CO), BF16),
        in_specs=[
            pl.BlockSpec((4, 3 * WR * WC, 128), lambda i: (0, 0, 0)),
            pl.BlockSpec((9 * CO, CH), lambda i: (0, 0)),
            pl.BlockSpec((1, CO), lambda i: (0, 0)),
            pl.BlockSpec((UROWS, depth), lambda i: (i, 0)),
            pl.BlockSpec((TW, depth), lambda i: (0, 0)),
        ],
        out_specs=pl.BlockSpec((3, 1, UROWS * TW, CO), lambda i: (0, 0, i, 0)),
        scratch_shapes=[pltpu.VMEM((depth, 3 * CO), BF16)],
        compiler_params=pltpu.CompilerParams(vmem_limit_bytes=40 * 2**20),
        name="convolve",
    )(win, weight, bias, row_part, col_part)


def spread_parts(tile_row, tile_col):
    lane = jnp.arange(9 * WR * WC, dtype=jnp.int32)[None, :]
    pixel = jnp.arange(TH, dtype=jnp.int32)[:, None]
    row_pos = tile_row * TH - 1 + lane // (3 * WR * WC) + pixel
    row_node = 4 * tile_row - 1 + (lane // WC) % WR
    col_pos = tile_col * TW - 1 + (lane // (WR * WC)) % 3 + pixel
    col_node = 6 * tile_col - 1 + lane % WC
    rows = bilinear(row_pos, 2 * BR, FN, row_node)
    cols = bilinear(col_pos, 2 * BC, FN, col_node)
    return rows, cols


def on_device(coarse, region_lat, region_lon, region_order, conv_weight, conv_bias):
    band = lax.axis_index("band")
    own = coarse[0]
    other = lax.ppermute(own, "band", [(i, i ^ 1) for i in range(64)])
    table, chips, places, branch = plan(region_lat, region_lon, region_order)
    planes = [[2 * m + c for m in range(32)] for c in range(2)]

    def route(capacity):
        def run(own, other, table, chips, places):
            cut = pick(capacity, table, own, other)
            got = lax.all_to_all(cut, "band", 0, 0, axis_index_groups=planes)
            return regroup(capacity, chips, places, got)

        return run

    tiles = lax.switch(
        branch[0], [route(cap) for cap in CAPACITIES], own, other, table, chips, places
    )
    win = lax.all_to_all(tiles.reshape(4, 3 * WR * WC, 128), "grp", 0, 0)
    rows, cols = spread_parts(band // TCOLS, band % TCOLS)
    weight = conv_weight.reshape(9 * CO, CH)
    return jnp.swapaxes(convolve(win, weight, conv_bias[None, :], rows, cols), 2, 3)


def solution(mesh):
    in_specs = (P("band", "grp", None, None), P(), P(), P(), P(), P())
    out_specs = P("grp", "band", None, None)
    return jax.shard_map(
        on_device, mesh=mesh, in_specs=in_specs, out_specs=out_specs, check_vma=False
    )
```

```python
import functools

import jax
import jax.numpy as jnp
from jax import lax
from jax.experimental import pallas as pl
from jax.experimental.layout import Layout, with_layout_constraint
from jax.experimental.pallas import tpu as pltpu
from jax.sharding import PartitionSpec as P

CH = 73
CO = 128
FN = 448
BR = 16
BC = 24
CELLS = BR * BC
TCOLS = 8
TH = 56
TW = 56
WR = 6
WC = 8
MAIN = 64
REST = CH - MAIN
ROW = 64
NEAR = 3
DEPTH = 256
UROWS = 14
CAPACITIES = (1, 2, 3, 4, 12)
F32 = jnp.float32
BF16 = jnp.bfloat16


def bilinear(positions, node_count, fine_count, nodes):
    coords = (positions.astype(F32) + 0.5) * (node_count / fine_count) - 0.5
    coords = jnp.clip(coords, 0.0, node_count - 1.0)
    weight = jnp.maximum(0.0, 1.0 - jnp.abs(coords - nodes.astype(F32)))
    inside = (positions >= 0) & (positions < fine_count)
    return jnp.where(inside, weight, 0.0)


def plan_kernel(lat, lon, order, table, chips, places, branch, counts):
    band, group = lax.axis_index("band"), lax.axis_index("grp")
    chip, core = lax.shift_right_logical(band, 1), lax.bitwise_and(band, 1)
    spot = lax.broadcasted_iota(jnp.int32, (8, 128), 1)
    spot_m, spot_g = lax.bitwise_and(spot, 31), lax.shift_right_logical(spot, 5)
    tally = jnp.zeros((8, 128), jnp.int32)
    for n in range(48):
        table[n] = -1
    held = []
    for i in range(12):
        region = order[i]
        lat0, lon0 = lat[region], lon[region]
        lon1 = jnp.where(lon0 == 59, 0, lon0 + 1)
        m0, m1 = lax.shift_right_logical(lat0, 1), lax.shift_right_logical(lat0 + 1, 1)
        g0, g1 = [
            (x >= 15).astype(jnp.int32) + (x >= 30).astype(jnp.int32) + (x >= 45).astype(jnp.int32)
            for x in (lon0, lon1)
        ]
        meets = ((spot_m == m0) | (spot_m == m1)) & ((spot_g == g0) | (spot_g == g1))
        tally = tally + meets.astype(jnp.int32)
        counts[m0] = 0
        counts[m1] = 0
        chips[2 * i] = m0
        chips[2 * i + 1] = m1
        held.append((lat0, lon0, lon1, m0, m1, (g0 == group) | (g1 == group)))
    counts[chip] = 0
    for i, (lat0, lon0, lon1, m0, m1, here) in enumerate(held):
        one = here.astype(jnp.int32)
        two = (here & (m0 != m1)).astype(jnp.int32)
        q = counts[chip]
        n0 = counts[m0]
        places[2 * i] = jnp.where(here, n0, -1)
        counts[m0] = n0 + one
        n1 = counts[m1]
        places[2 * i + 1] = jnp.where(two == 1, n1, -1)
        counts[m1] = n1 + two

        @pl.when(here & ((m0 == chip) | (m1 == chip)))
        def _():
            for j in range(2):
                row = lat0 + j - 2 * chip
                for k, at in enumerate((lon0, lon1)):
                    col = at - 15 * group
                    ok = (row >= 0) & (row < 2) & (col >= 0) & (col < 15)
                    side = jnp.where(row == core, 0, 16)
                    table[q * 4 + j * 2 + k] = jnp.where(ok, side + col, -1)

    most = jnp.max(tally)
    step = jnp.int32(0)
    for cap in CAPACITIES[:-1]:
        step = step + (most > cap).astype(jnp.int32)
    branch[0] = step


def plan(lat, lon, order):
    smem = pl.BlockSpec(memory_space=pltpu.SMEM)
    return pl.pallas_call(
        plan_kernel,
        out_shape=[jax.ShapeDtypeStruct((n,), jnp.int32) for n in (48, 24, 24, 1)],
        in_specs=[smem] * 3,
        out_specs=[smem] * 4,
        scratch_shapes=[pltpu.SMEM((33,), jnp.int32)],
        name="plan",
    )(lat, lon, order)


def payload_rows(capacity):
    return 24 * capacity + 8 * ((capacity + 1) // 2)


def pick_kernel(capacity, table, own, other, out, window, blocks):
    core = lax.rem(lax.axis_index("band"), 2)
    lane = lax.broadcasted_iota(jnp.int32, (8, 128), 1)
    turn = (
        lax.broadcasted_iota(jnp.int32, (128, 128), 0)
        == lax.broadcasted_iota(jnp.int32, (128, 128), 1)
    ).astype(BF16)
    zeros = jnp.zeros((ROW, 128), F32)
    for n in range(4 * capacity):
        code = table[n]

        @pl.when(code < 0)
        def _():
            blocks[n * 128 : (n + 1) * 128] = jnp.zeros((128, CELLS), BF16)

        @pl.when((code >= 0) & (code < 16))
        def _():
            blocks[n * 128 : n * 128 + CH] = own[code]

        @pl.when(code >= 16)
        def _():
            blocks[n * 128 : n * 128 + CH] = other[code - 16]

    for q in range(capacity):
        base = q * 34 * ROW
        window[base : base + ROW] = zeros
        window[base + 33 * ROW : base + 34 * ROW] = zeros
        for r in range(1, 33):
            window[base + r * ROW : base + r * ROW + 8] = zeros[:8]
            window[base + r * ROW + 56 : base + r * ROW + 64] = zeros[:8]
        turned = jnp.concatenate(
            [
                lax.dot_general(
                    turn,
                    blocks[512 * q : 512 * q + 512, 128 * i : 128 * i + 128],
                    (((1,), (1,)), ((), ())),
                    preferred_element_type=F32,
                )
                for i in range(3)
            ],
            axis=0,
        )
        for j in range(2):
            for k in range(2):
                n = 2 * j + k
                for r in range(BR):
                    at = base + (16 * j + r + 1) * ROW + 8 + BC * k
                    window[at : at + BC] = turned[
                        r * BC : (r + 1) * BC, n * 128 : (n + 1) * 128
                    ]

    def emit(a, carry):
        for b in range(4):
            mains, rests = [], []
            for q in range(capacity):
                rows = []
                for i in range(WR):
                    at = q * 34 * ROW + i * ROW + 7 + 12 * b + 6 * core + a * 4 * ROW
                    rows.append(window[pl.ds(at, WC)])
                for i in range(3):
                    mains.append(
                        jnp.where(lane < MAIN, rows[i], pltpu.roll(rows[i + 3], MAIN, 1))
                    )
                side = 64 * (q % 2)
                rest = jnp.zeros((8, 128), F32)
                for i in range(WR):
                    lo = side + REST * i
                    moved = pltpu.roll(rows[i], (lo - MAIN) % 128, 1)
                    rest = jnp.where((lane >= lo) & (lane < lo + REST), moved, rest)
                if q % 2 == 0:
                    rests.append(rest)
                else:
                    rests[-1] = rests[-1] + rest
            out[4 * a + b] = jnp.concatenate(mains + rests, axis=0).astype(BF16)
        return carry

    lax.fori_loop(0, 8, emit, 0, unroll=8 if capacity <= 2 else 1)


def pick(capacity, table, own, other):
    vmem = pl.BlockSpec(memory_space=pltpu.VMEM)
    smem = pl.BlockSpec(memory_space=pltpu.SMEM)
    return pl.pallas_call(
        functools.partial(pick_kernel, capacity),
        out_shape=jax.ShapeDtypeStruct((32, payload_rows(capacity), 128), BF16),
        in_specs=[smem, vmem, vmem],
        out_specs=vmem,
        scratch_shapes=[
            pltpu.VMEM((capacity * 34 * ROW, 128), F32),
            pltpu.VMEM((capacity * 4 * 128, CELLS), BF16),
        ],
        compiler_params=pltpu.CompilerParams(vmem_limit_bytes=40 * 2**20),
        name="pick",
    )(table, own, other)


def regroup_kernel(capacity, chips, places, got, *outs):
    group = lax.axis_index("grp")
    lane = lax.broadcasted_iota(jnp.int32, (8, 128), 1)
    def gather(out, hop, s):
        slot = lax.bitwise_and(group + hop, 3) * 3 + s
        main = jnp.zeros((24, 128), F32)
        rest = jnp.zeros((8, 128), F32)
        for j in range(2):
            place = places[slot * 2 + j]
            part = got[chips[slot * 2 + j]].astype(F32)
            for q in range(capacity):
                here = place == q
                main = main + jnp.where(here, part[24 * q : 24 * q + 24], 0.0)
                at = 24 * capacity + 8 * (q // 2)
                side = part[at : at + 8]
                if q % 2:
                    side = pltpu.roll(side, 64, 1)
                rest = rest + jnp.where(here, side, 0.0)
        rows = []
        for i in range(WR):
            body = main[8 * (i % 3) : 8 * (i % 3) + 8]
            if i >= 3:
                body = pltpu.roll(body, 64, 1)
            tail = pltpu.roll(rest, (MAIN - REST * i) % 128, 1)
            row = jnp.where(lane < MAIN, body, jnp.where(lane < CH, tail, 0.0))
            rows.append(row)
        out[WR * WC * s : WR * WC * (s + 1)] = jnp.concatenate(rows, axis=0).astype(BF16)

    for hop in range(4):
        for s in range(3):
            gather(outs[hop], hop, s)


def regroup(capacity, chips, places, got):
    vmem = pl.BlockSpec(memory_space=pltpu.VMEM)
    smem = pl.BlockSpec(memory_space=pltpu.SMEM)
    return pl.pallas_call(
        functools.partial(regroup_kernel, capacity),
        out_shape=[jax.ShapeDtypeStruct((3 * WR * WC, 128), BF16)] * 4,
        in_specs=[smem, smem, vmem],
        out_specs=[vmem] * 4,
        compiler_params=pltpu.CompilerParams(vmem_limit_bytes=24 * 2**20),
        name="regroup",
    )(chips, places, got)


def conv_kernel(win0, win1, win2, win3, weight, bias, row_part, col_part, out, taps):
    step = pl.program_id(0)
    n = WR * WC

    @pl.when(step == 0)
    def _():
        cells = win0[...].astype(F32) + win1[...].astype(F32)
        cells = cells + (win2[...].astype(F32) + win3[...].astype(F32))
        cells = cells.astype(BF16)[:, :CH]
        every = jnp.concatenate([weight[t] for t in range(9)], axis=1)
        made = jnp.dot(cells, every, preferred_element_type=F32) * 0.5
        for t in range(9):
            for s in range(3):
                taps[t * n : (t + 1) * n, s * CO : (s + 1) * CO] = made[
                    s * n : (s + 1) * n, t * CO : (t + 1) * CO
                ]

    near = [
        taps[pl.ds(pl.multiple_of(t * n + WC * step, 8), NEAR * WC)] for t in range(9)
    ]
    near.append(jnp.zeros((DEPTH - 9 * NEAR * WC, 3 * CO), F32))
    near = jnp.concatenate(near, axis=0).astype(BF16)
    cols = col_part[...]
    spread = jnp.concatenate(
        [cols * row_part[pl.ds(step * UROWS + u, 1)] for u in range(UROWS)], axis=0
    ).astype(BF16)
    half = jnp.dot(spread, near, preferred_element_type=F32)
    for s in range(3):
        h = half[:, s * CO : (s + 1) * CO] + 0.5 * bias[...]
        out[s, 0] = (h + h * jnp.tanh(h)).astype(BF16)


def convolve(wins, weight, bias, row_part, col_part):
    whole = pl.BlockSpec(memory_space=pltpu.VMEM)
    return pl.pallas_call(
        conv_kernel,
        grid=(TH // UROWS,),
        out_shape=jax.ShapeDtypeStruct((3, 1, TH * TW, CO), BF16),
        in_specs=[whole] * 8,
        out_specs=pl.BlockSpec((3, 1, UROWS * TW, CO), lambda i: (0, 0, i, 0)),
        scratch_shapes=[pltpu.VMEM((9 * WR * WC, 3 * CO), F32)],
        compiler_params=pltpu.CompilerParams(vmem_limit_bytes=40 * 2**20),
        name="convolve",
    )(*wins, weight, bias, row_part, col_part)


def spread_parts(tile_row, tile_col):
    lane = jnp.arange(DEPTH, dtype=jnp.int32)[None, :]
    pixel = jnp.arange(TH, dtype=jnp.int32)[:, None]
    row_pos = tile_row * TH - 1 + lane // (3 * NEAR * WC) + pixel
    row_node = 4 * tile_row - 1 + pixel // UROWS + (lane // WC) % NEAR
    col_pos = tile_col * TW - 1 + (lane // (NEAR * WC)) % 3 + pixel
    col_node = 6 * tile_col - 1 + lane % WC
    rows = bilinear(row_pos, 2 * BR, FN, row_node)
    cols = bilinear(col_pos, 2 * BC, FN, col_node)
    return rows, cols


def on_device(coarse, region_lat, region_lon, region_order, conv_weight, conv_bias):
    band = lax.axis_index("band")
    own = coarse[0]
    other = lax.ppermute(own, "band", [(i, i ^ 1) for i in range(64)])
    table, chips, places, branch = plan(region_lat, region_lon, region_order)
    branch = jnp.clip(branch[0], 0, len(CAPACITIES) - 1)
    own, table, branch = lax.optimization_barrier((own, table, branch))
    own = with_layout_constraint(own, Layout(major_to_minor=(0, 1, 2)))
    planes = [[2 * m + c for m in range(32)] for c in range(2)]

    def route(capacity):
        def run(own, other, table, chips, places):
            cut = pick(capacity, table, own, other)
            got = lax.all_to_all(cut, "band", 0, 0, axis_index_groups=planes)
            return regroup(capacity, chips, places, got)

        return run

    tiles = lax.switch(
        branch, [route(cap) for cap in CAPACITIES], own, other, table, chips, places
    )
    band, *tiles = lax.optimization_barrier((band, *tiles))
    wins = [tiles[0]] + [
        lax.ppermute(tiles[hop], "grp", [(i, (i + hop) % 4) for i in range(4)])
        for hop in (2, 1, 3)
    ]
    rows, cols = spread_parts(band // TCOLS, band % TCOLS)
    weight = jnp.swapaxes(conv_weight, 1, 2)
    return jnp.swapaxes(convolve(wins, weight, conv_bias[None, :], rows, cols), 2, 3)


def solution(mesh):
    in_specs = (P("band", "grp", None, None), P(), P(), P(), P(), P())
    out_specs = P("grp", "band", None, None)
    return jax.shard_map(
        on_device, mesh=mesh, in_specs=in_specs, out_specs=out_specs, check_vma=False
    )
```

```python
import functools

import jax
import jax.numpy as jnp
from jax import lax
from jax.experimental import pallas as pl
from jax.experimental.layout import Layout, with_layout_constraint
from jax.experimental.pallas import tpu as pltpu
from jax.sharding import PartitionSpec as P

CH = 73
CO = 128
FN = 448
BR = 16
BC = 24
CELLS = BR * BC
TCOLS = 8
TH = 56
TW = 56
WR = 6
WC = 8
MAIN = 64
REST = CH - MAIN
ROW = 64
NEAR = 3
DEPTH = 256
UROWS = 14
SPARE = 48
CHIPS = 56
PLACES = 80
HELD = 104
CAPACITIES = (1, 2, 3, 4, 12)
F32 = jnp.float32
BF16 = jnp.bfloat16


def bilinear(positions, node_count, fine_count, nodes):
    coords = (positions.astype(F32) + 0.5) * (node_count / fine_count) - 0.5
    coords = jnp.clip(coords, 0.0, node_count - 1.0)
    weight = jnp.maximum(0.0, 1.0 - jnp.abs(coords - nodes.astype(F32)))
    inside = (positions >= 0) & (positions < fine_count)
    return jnp.where(inside, weight, 0.0)


def plan_kernel(lat, lon, order, tables, branch, counts):
    band, group = lax.axis_index("band"), lax.axis_index("grp")
    chip, core = lax.shift_right_logical(band, 1), lax.bitwise_and(band, 1)
    spot = lax.broadcasted_iota(jnp.int32, (8, 128), 1)
    spot_m, spot_g = lax.bitwise_and(spot, 31), lax.shift_right_logical(spot, 5)
    tally = jnp.zeros((8, 128), jnp.int32)
    held = []
    for i in range(12):
        region = order[i]
        lat0, lon0 = lat[region], lon[region]
        lon1 = jnp.where(lon0 == 59, 0, lon0 + 1)
        m0, m1 = lax.shift_right_logical(lat0, 1), lax.shift_right_logical(lat0 + 1, 1)
        g0, g1 = [
            (x >= 15).astype(jnp.int32) + (x >= 30).astype(jnp.int32) + (x >= 45).astype(jnp.int32)
            for x in (lon0, lon1)
        ]
        meets = ((spot_m == m0) | (spot_m == m1)) & ((spot_g == g0) | (spot_g == g1))
        tally = tally + meets.astype(jnp.int32)
        counts[m0] = 0
        counts[m1] = 0
        tables[CHIPS + 2 * i] = m0
        tables[CHIPS + 2 * i + 1] = m1
        held.append((lat0, lon0, lon1, m0, m1, (g0 == group) | (g1 == group)))
    most = jnp.max(tally)
    step = jnp.int32(0)
    for cap in CAPACITIES[:-1]:
        step = step + (most > cap).astype(jnp.int32)
    branch[0] = step
    q = jnp.int32(0)
    for i, (lat0, lon0, lon1, m0, m1, here) in enumerate(held):
        one = here.astype(jnp.int32)
        two = jnp.where(m0 != m1, one, 0)
        n0 = counts[m0]
        counts[m0] = n0 + one
        n1 = counts[m1]
        counts[m1] = n1 + two
        tables[PLACES + 2 * i] = jnp.where(here, n0, -1)
        tables[PLACES + 2 * i + 1] = jnp.where(two == 1, n1, -1)
        mine = here & ((m0 == chip) | (m1 == chip))
        at = jnp.where(mine, 4 * q, SPARE)
        for j in range(2):
            row = lat0 + j - 2 * chip
            side = jnp.where(row == core, 0, 16)
            for k, place in enumerate((lon0, lon1)):
                col = place - 15 * group
                ok = (row >= 0) & (row < 2) & (col >= 0) & (col < 15)
                tables[at + 2 * j + k] = jnp.where(ok, side + col, -1)
        q = q + mine.astype(jnp.int32)
    tables[HELD] = q


def plan(lat, lon, order):
    smem = pl.BlockSpec(memory_space=pltpu.SMEM)
    return pl.pallas_call(
        plan_kernel,
        out_shape=[jax.ShapeDtypeStruct((n,), jnp.int32) for n in (128, 1)],
        in_specs=[smem] * 3,
        out_specs=[smem] * 2,
        scratch_shapes=[pltpu.SMEM((33,), jnp.int32)],
        name="plan",
    )(lat, lon, order)


def payload_rows(capacity):
    return 24 * capacity + 8 * ((capacity + 1) // 2)


def pick_kernel(capacity, tables, own, other, out, window, blocks):
    core = lax.rem(lax.axis_index("band"), 2)
    lane = lax.broadcasted_iota(jnp.int32, (8, 128), 1)
    turn = (
        lax.broadcasted_iota(jnp.int32, (128, 128), 0)
        == lax.broadcasted_iota(jnp.int32, (128, 128), 1)
    ).astype(BF16)
    zeros = jnp.zeros((ROW, 128), F32)
    for n in range(4 * capacity):
        code = jnp.where(n // 4 < tables[HELD], tables[n], -1)

        @pl.when(code < 0)
        def _():
            blocks[n * 128 : (n + 1) * 128] = jnp.zeros((128, CELLS), BF16)

        @pl.when((code >= 0) & (code < 16))
        def _():
            blocks[n * 128 : n * 128 + CH] = own[code]

        @pl.when(code >= 16)
        def _():
            blocks[n * 128 : n * 128 + CH] = other[code - 16]

    for q in range(capacity):
        base = q * 34 * ROW
        window[base : base + ROW] = zeros
        window[base + 33 * ROW : base + 34 * ROW] = zeros
        for r in range(1, 33):
            window[base + r * ROW : base + r * ROW + 8] = zeros[:8]
            window[base + r * ROW + 56 : base + r * ROW + 64] = zeros[:8]
        turned = jnp.concatenate(
            [
                lax.dot_general(
                    turn,
                    blocks[512 * q : 512 * q + 512, 128 * i : 128 * i + 128],
                    (((1,), (1,)), ((), ())),
                    preferred_element_type=F32,
                )
                for i in range(3)
            ],
            axis=0,
        )
        for j in range(2):
            for k in range(2):
                n = 2 * j + k
                for r in range(BR):
                    at = base + (16 * j + r + 1) * ROW + 8 + BC * k
                    window[at : at + BC] = turned[
                        r * BC : (r + 1) * BC, n * 128 : (n + 1) * 128
                    ]

    def emit(a, carry):
        for b in range(4):
            mains, rests = [], []
            for q in range(capacity):
                rows = []
                for i in range(WR):
                    at = q * 34 * ROW + i * ROW + 7 + 12 * b + 6 * core + a * 4 * ROW
                    rows.append(window[pl.ds(at, WC)])
                for i in range(3):
                    mains.append(
                        jnp.where(lane < MAIN, rows[i], pltpu.roll(rows[i + 3], MAIN, 1))
                    )
                side = 64 * (q % 2)
                rest = jnp.zeros((8, 128), F32)
                for i in range(WR):
                    lo = side + REST * i
                    moved = pltpu.roll(rows[i], (lo - MAIN) % 128, 1)
                    rest = jnp.where((lane >= lo) & (lane < lo + REST), moved, rest)
                if q % 2 == 0:
                    rests.append(rest)
                else:
                    rests[-1] = rests[-1] + rest
            out[4 * a + b] = jnp.concatenate(mains + rests, axis=0).astype(BF16)
        return carry

    lax.fori_loop(0, 8, emit, 0, unroll=8 if capacity <= 2 else 1)


def pick(capacity, tables, own, other):
    vmem = pl.BlockSpec(memory_space=pltpu.VMEM)
    smem = pl.BlockSpec(memory_space=pltpu.SMEM)
    return pl.pallas_call(
        functools.partial(pick_kernel, capacity),
        out_shape=jax.ShapeDtypeStruct((32, payload_rows(capacity), 128), BF16),
        in_specs=[smem, vmem, vmem],
        out_specs=vmem,
        scratch_shapes=[
            pltpu.VMEM((capacity * 34 * ROW, 128), F32),
            pltpu.VMEM((capacity * 4 * 128, CELLS), BF16),
        ],
        compiler_params=pltpu.CompilerParams(vmem_limit_bytes=40 * 2**20),
        name="pick",
    )(tables, own, other)


def regroup_kernel(capacity, tables, got, *outs):
    group = lax.axis_index("grp")
    lane = lax.broadcasted_iota(jnp.int32, (8, 128), 1)
    def gather(out, hop, s):
        slot = lax.bitwise_and(group + hop, 3) * 3 + s
        main = jnp.zeros((24, 128), F32)
        rest = jnp.zeros((8, 128), F32)
        for j in range(2):
            place = tables[PLACES + slot * 2 + j]
            part = got[tables[CHIPS + slot * 2 + j]].astype(F32)
            for q in range(capacity):
                here = place == q
                main = main + jnp.where(here, part[24 * q : 24 * q + 24], 0.0)
                at = 24 * capacity + 8 * (q // 2)
                side = part[at : at + 8]
                if q % 2:
                    side = pltpu.roll(side, 64, 1)
                rest = rest + jnp.where(here, side, 0.0)
        rows = []
        for i in range(WR):
            body = main[8 * (i % 3) : 8 * (i % 3) + 8]
            if i >= 3:
                body = pltpu.roll(body, 64, 1)
            tail = pltpu.roll(rest, (MAIN - REST * i) % 128, 1)
            row = jnp.where(lane < MAIN, body, jnp.where(lane < CH, tail, 0.0))
            rows.append(row)
        out[WR * WC * s : WR * WC * (s + 1)] = jnp.concatenate(rows, axis=0).astype(BF16)

    for hop in range(4):
        for s in range(3):
            gather(outs[hop], hop, s)


def regroup(capacity, tables, got):
    vmem = pl.BlockSpec(memory_space=pltpu.VMEM)
    smem = pl.BlockSpec(memory_space=pltpu.SMEM)
    return pl.pallas_call(
        functools.partial(regroup_kernel, capacity),
        out_shape=[jax.ShapeDtypeStruct((3 * WR * WC, 128), BF16)] * 4,
        in_specs=[smem, vmem],
        out_specs=[vmem] * 4,
        compiler_params=pltpu.CompilerParams(vmem_limit_bytes=24 * 2**20),
        name="regroup",
    )(tables, got)


def conv_kernel(win0, win1, win2, win3, weight, bias, spread, out, taps, result, sems):
    n = WR * WC
    cells = win0[...].astype(F32) + win1[...].astype(F32)
    cells = cells + (win2[...].astype(F32) + win3[...].astype(F32))
    cells = cells.astype(BF16)[:, :CH]
    every = jnp.concatenate([weight[t] for t in range(9)], axis=1)
    made = jnp.dot(cells, every, preferred_element_type=F32) * 0.5
    for t in range(9):
        for s in range(3):
            taps[t * n : (t + 1) * n, s * CO : (s + 1) * CO] = made[
                s * n : (s + 1) * n, t * CO : (t + 1) * CO
            ]
    half_bias = 0.5 * bias[...]
    size = UROWS * TW
    sent = []
    for step in range(TH // UROWS):
        near = [
            taps[t * n + WC * step : t * n + WC * (step + NEAR)] for t in range(9)
        ]
        near.append(jnp.zeros((DEPTH - 9 * NEAR * WC, 3 * CO), F32))
        near = jnp.concatenate(near, axis=0).astype(BF16)
        part = slice(step * size, (step + 1) * size)
        half = jnp.dot(spread[part], near, preferred_element_type=F32)
        for s in range(3):
            h = half[:, s * CO : (s + 1) * CO] + half_bias
            result[s, part] = (h + h * jnp.tanh(h)).astype(BF16)
        rows = pl.ds(step * size, size)
        sent.append(
            pltpu.make_async_copy(result.at[:, rows], out.at[:, 0, rows], sems.at[step])
        )
        sent[-1].start()
    for copy in sent:
        copy.wait()


def convolve(wins, weight, bias, spread):
    whole = pl.BlockSpec(memory_space=pltpu.VMEM)
    return pl.pallas_call(
        conv_kernel,
        out_shape=jax.ShapeDtypeStruct((3, 1, TH * TW, CO), BF16),
        in_specs=[whole] * 7,
        out_specs=pl.BlockSpec(memory_space=pl.ANY),
        scratch_shapes=[
            pltpu.VMEM((9 * WR * WC, 3 * CO), F32),
            pltpu.VMEM((3, TH * TW, CO), BF16),
            pltpu.SemaphoreType.DMA((TH // UROWS,)),
        ],
        compiler_params=pltpu.CompilerParams(vmem_limit_bytes=40 * 2**20),
        name="convolve",
    )(*wins, weight, bias, spread)


def spread_matrix(tile_row, tile_col):
    lane = jnp.arange(DEPTH, dtype=jnp.int32)[None, :]
    pixel = jnp.arange(TH, dtype=jnp.int32)[:, None]
    row_pos = tile_row * TH - 1 + lane // (3 * NEAR * WC) + pixel
    row_node = 4 * tile_row - 1 + pixel // UROWS + (lane // WC) % NEAR
    col_pos = tile_col * TW - 1 + (lane // (NEAR * WC)) % 3 + pixel
    col_node = 6 * tile_col - 1 + lane % WC
    rows = bilinear(row_pos, 2 * BR, FN, row_node)
    cols = bilinear(col_pos, 2 * BC, FN, col_node)
    return (rows[:, None, :] * cols[None, :, :]).astype(BF16).reshape(TH * TW, DEPTH)


def on_device(coarse, region_lat, region_lon, region_order, conv_weight, conv_bias):
    band = lax.axis_index("band")
    own = coarse[0]
    other = lax.ppermute(own, "band", [(i, i ^ 1) for i in range(64)])
    own = with_layout_constraint(own, Layout(major_to_minor=(0, 1, 2)))
    tables, branch = plan(region_lat, region_lon, region_order)
    planes = [[2 * m + c for m in range(32)] for c in range(2)]

    def route(capacity):
        def run(own, other, tables):
            cut = pick(capacity, tables, own, other)
            got = lax.all_to_all(cut, "band", 0, 0, axis_index_groups=planes)
            return regroup(capacity, tables, got)

        return run

    tiles = lax.switch(branch[0], [route(cap) for cap in CAPACITIES], own, other, tables)
    band, *tiles = lax.optimization_barrier((band, *tiles))
    wins = [tiles[0]] + [
        lax.ppermute(tiles[hop], "grp", [(i, (i + hop) % 4) for i in range(4)])
        for hop in (2, 1, 3)
    ]
    spread = spread_matrix(band // TCOLS, band % TCOLS)
    weight = jnp.swapaxes(conv_weight, 1, 2)
    return jnp.swapaxes(convolve(wins, weight, conv_bias[None, :], spread), 2, 3)


def solution(mesh):
    in_specs = (P("band", "grp", None, None), P(), P(), P(), P(), P())
    out_specs = P("grp", "band", None, None)
    return jax.shard_map(
        on_device, mesh=mesh, in_specs=in_specs, out_specs=out_specs, check_vma=False
    )
```

```python
import functools

import jax
import jax.numpy as jnp
from jax import lax
from jax.experimental import pallas as pl
from jax.experimental.layout import Layout, with_layout_constraint
from jax.experimental.pallas import tpu as pltpu
from jax.sharding import PartitionSpec as P

CH = 73
CO = 128
FN = 448
BR = 16
BC = 24
CELLS = BR * BC
TCOLS = 8
TH = 56
TW = 56
WR = 6
WC = 8
MAIN = 64
REST = CH - MAIN
ROW = 64
NEAR = 3
DEPTH = 256
UROWS = 14
SPARE = 48
CHIPS = 56
PLACES = 80
HELD = 104
CAPACITIES = (1, 2, 3, 4, 12)
F32 = jnp.float32
BF16 = jnp.bfloat16


def bilinear(positions, node_count, fine_count, nodes):
    coords = (positions.astype(F32) + 0.5) * (node_count / fine_count) - 0.5
    coords = jnp.clip(coords, 0.0, node_count - 1.0)
    weight = jnp.maximum(0.0, 1.0 - jnp.abs(coords - nodes.astype(F32)))
    inside = (positions >= 0) & (positions < fine_count)
    return jnp.where(inside, weight, 0.0)


def rank_of(chip):
    return lax.bitwise_and(chip, 7) * 4 + lax.shift_right_logical(chip, 3)


def plan_kernel(lat, lon, order, tables, branch, counts):
    band, group = lax.axis_index("band"), lax.axis_index("grp")
    chip, core = lax.shift_right_logical(band, 1), lax.bitwise_and(band, 1)
    spot = lax.broadcasted_iota(jnp.int32, (8, 128), 1)
    spot_m, spot_g = lax.bitwise_and(spot, 31), lax.shift_right_logical(spot, 5)
    tally = jnp.zeros((8, 128), jnp.int32)
    held = []
    for i in range(12):
        region = order[i]
        lat0, lon0 = lat[region], lon[region]
        lon1 = jnp.where(lon0 == 59, 0, lon0 + 1)
        m0, m1 = lax.shift_right_logical(lat0, 1), lax.shift_right_logical(lat0 + 1, 1)
        g0, g1 = [
            (x >= 15).astype(jnp.int32) + (x >= 30).astype(jnp.int32) + (x >= 45).astype(jnp.int32)
            for x in (lon0, lon1)
        ]
        meets = ((spot_m == m0) | (spot_m == m1)) & ((spot_g == g0) | (spot_g == g1))
        tally = tally + meets.astype(jnp.int32)
        counts[m0] = 0
        counts[m1] = 0
        tables[CHIPS + 2 * i] = rank_of(m0)
        tables[CHIPS + 2 * i + 1] = rank_of(m1)
        held.append((lat0, lon0, lon1, m0, m1, (g0 == group) | (g1 == group)))
    most = jnp.max(tally)
    step = jnp.int32(0)
    for cap in CAPACITIES[:-1]:
        step = step + (most > cap).astype(jnp.int32)
    branch[0] = step
    q = jnp.int32(0)
    for i, (lat0, lon0, lon1, m0, m1, here) in enumerate(held):
        one = here.astype(jnp.int32)
        two = jnp.where(m0 != m1, one, 0)
        n0 = counts[m0]
        counts[m0] = n0 + one
        n1 = counts[m1]
        counts[m1] = n1 + two
        tables[PLACES + 2 * i] = jnp.where(here, n0, -1)
        tables[PLACES + 2 * i + 1] = jnp.where(two == 1, n1, -1)
        mine = here & ((m0 == chip) | (m1 == chip))
        at = jnp.where(mine, 4 * q, SPARE)
        for j in range(2):
            row = lat0 + j - 2 * chip
            side = jnp.where(row == core, 0, 16)
            for k, place in enumerate((lon0, lon1)):
                col = place - 15 * group
                ok = (row >= 0) & (row < 2) & (col >= 0) & (col < 15)
                tables[at + 2 * j + k] = jnp.where(ok, side + col, -1)
        q = q + mine.astype(jnp.int32)
    tables[HELD] = q


def plan(lat, lon, order):
    smem = pl.BlockSpec(memory_space=pltpu.SMEM)
    return pl.pallas_call(
        plan_kernel,
        out_shape=[jax.ShapeDtypeStruct((n,), jnp.int32) for n in (128, 1)],
        in_specs=[smem] * 3,
        out_specs=[smem] * 2,
        scratch_shapes=[pltpu.SMEM((33,), jnp.int32)],
        name="plan",
    )(lat, lon, order)


def payload_rows(capacity):
    return 24 * capacity + 8 * ((capacity + 1) // 2)


def pick_kernel(capacity, tables, own, other, out, window, blocks):
    core = lax.rem(lax.axis_index("band"), 2)
    lane = lax.broadcasted_iota(jnp.int32, (8, 128), 1)
    turn = (
        lax.broadcasted_iota(jnp.int32, (128, 128), 0)
        == lax.broadcasted_iota(jnp.int32, (128, 128), 1)
    ).astype(BF16)
    zeros = jnp.zeros((ROW, 128), F32)
    for n in range(4 * capacity):
        code = jnp.where(n // 4 < tables[HELD], tables[n], -1)

        @pl.when(code < 0)
        def _():
            blocks[n * 128 : (n + 1) * 128] = jnp.zeros((128, CELLS), BF16)

        @pl.when((code >= 0) & (code < 16))
        def _():
            blocks[n * 128 : n * 128 + CH] = own[code]

        @pl.when(code >= 16)
        def _():
            blocks[n * 128 : n * 128 + CH] = other[code - 16]

    for q in range(capacity):
        base = q * 34 * ROW
        window[base : base + ROW] = zeros
        window[base + 33 * ROW : base + 34 * ROW] = zeros
        for r in range(1, 33):
            window[base + r * ROW : base + r * ROW + 8] = zeros[:8]
            window[base + r * ROW + 56 : base + r * ROW + 64] = zeros[:8]
        turned = jnp.concatenate(
            [
                lax.dot_general(
                    turn,
                    blocks[512 * q : 512 * q + 512, 128 * i : 128 * i + 128],
                    (((1,), (1,)), ((), ())),
                    preferred_element_type=F32,
                )
                for i in range(3)
            ],
            axis=0,
        )
        for j in range(2):
            for k in range(2):
                n = 2 * j + k
                for r in range(BR):
                    at = base + (16 * j + r + 1) * ROW + 8 + BC * k
                    window[at : at + BC] = turned[
                        r * BC : (r + 1) * BC, n * 128 : (n + 1) * 128
                    ]

    def emit(a, carry):
        for b in range(4):
            mains, rests = [], []
            for q in range(capacity):
                rows = []
                for i in range(WR):
                    at = q * 34 * ROW + i * ROW + 7 + 12 * b + 6 * core + a * 4 * ROW
                    rows.append(window[pl.ds(at, WC)])
                for i in range(3):
                    mains.append(
                        jnp.where(lane < MAIN, rows[i], pltpu.roll(rows[i + 3], MAIN, 1))
                    )
                side = 64 * (q % 2)
                rest = jnp.zeros((8, 128), F32)
                for i in range(WR):
                    lo = side + REST * i
                    moved = pltpu.roll(rows[i], (lo - MAIN) % 128, 1)
                    rest = jnp.where((lane >= lo) & (lane < lo + REST), moved, rest)
                if q % 2 == 0:
                    rests.append(rest)
                else:
                    rests[-1] = rests[-1] + rest
            chip = 4 * a + b
            out[rank_of(chip)] = jnp.concatenate(mains + rests, axis=0).astype(BF16)
        return carry

    lax.fori_loop(0, 8, emit, 0, unroll=8 if capacity <= 2 else 1)


def pick(capacity, tables, own, other):
    vmem = pl.BlockSpec(memory_space=pltpu.VMEM)
    smem = pl.BlockSpec(memory_space=pltpu.SMEM)
    return pl.pallas_call(
        functools.partial(pick_kernel, capacity),
        out_shape=jax.ShapeDtypeStruct((32, payload_rows(capacity), 128), BF16),
        in_specs=[smem, vmem, vmem],
        out_specs=vmem,
        scratch_shapes=[
            pltpu.VMEM((capacity * 34 * ROW, 128), F32),
            pltpu.VMEM((capacity * 4 * 128, CELLS), BF16),
        ],
        compiler_params=pltpu.CompilerParams(vmem_limit_bytes=40 * 2**20),
        name="pick",
    )(tables, own, other)


def regroup_kernel(capacity, tables, got, *outs):
    group = lax.axis_index("grp")
    lane = lax.broadcasted_iota(jnp.int32, (8, 128), 1)
    def gather(out, hop, s):
        slot = lax.bitwise_and(group + hop, 3) * 3 + s
        main = jnp.zeros((24, 128), F32)
        rest = jnp.zeros((8, 128), F32)
        for j in range(2):
            place = tables[PLACES + slot * 2 + j]
            part = got[tables[CHIPS + slot * 2 + j]].astype(F32)
            for q in range(capacity):
                here = place == q
                main = main + jnp.where(here, part[24 * q : 24 * q + 24], 0.0)
                at = 24 * capacity + 8 * (q // 2)
                side = part[at : at + 8]
                if q % 2:
                    side = pltpu.roll(side, 64, 1)
                rest = rest + jnp.where(here, side, 0.0)
        rows = []
        for i in range(WR):
            body = main[8 * (i % 3) : 8 * (i % 3) + 8]
            if i >= 3:
                body = pltpu.roll(body, 64, 1)
            tail = pltpu.roll(rest, (MAIN - REST * i) % 128, 1)
            row = jnp.where(lane < MAIN, body, jnp.where(lane < CH, tail, 0.0))
            rows.append(row)
        out[WR * WC * s : WR * WC * (s + 1)] = jnp.concatenate(rows, axis=0).astype(BF16)

    for hop in range(4):
        for s in range(3):
            gather(outs[hop], hop, s)


def regroup(capacity, tables, got):
    vmem = pl.BlockSpec(memory_space=pltpu.VMEM)
    smem = pl.BlockSpec(memory_space=pltpu.SMEM)
    return pl.pallas_call(
        functools.partial(regroup_kernel, capacity),
        out_shape=[jax.ShapeDtypeStruct((3 * WR * WC, 128), BF16)] * 4,
        in_specs=[smem, vmem],
        out_specs=[vmem] * 4,
        compiler_params=pltpu.CompilerParams(vmem_limit_bytes=24 * 2**20),
        name="regroup",
    )(tables, got)


def conv_kernel(win0, win1, win2, win3, weight, bias, spread, out, taps, result, sems):
    n = WR * WC
    cells = win0[...].astype(F32) + win1[...].astype(F32)
    cells = cells + (win2[...].astype(F32) + win3[...].astype(F32))
    cells = cells.astype(BF16)[:, :CH]
    every = jnp.concatenate([weight[t] for t in range(9)], axis=1)
    made = jnp.dot(cells, every, preferred_element_type=F32) * 0.5
    for t in range(9):
        for s in range(3):
            taps[t * n : (t + 1) * n, s * CO : (s + 1) * CO] = made[
                s * n : (s + 1) * n, t * CO : (t + 1) * CO
            ]
    half_bias = 0.5 * bias[...]
    size = UROWS * TW
    sent = []
    for step in range(TH // UROWS):
        near = [
            taps[t * n + WC * step : t * n + WC * (step + NEAR)] for t in range(9)
        ]
        near.append(jnp.zeros((DEPTH - 9 * NEAR * WC, 3 * CO), F32))
        near = jnp.concatenate(near, axis=0).astype(BF16)
        part = slice(step * size, (step + 1) * size)
        half = jnp.dot(spread[part], near, preferred_element_type=F32)
        for s in range(3):
            h = half[:, s * CO : (s + 1) * CO] + half_bias
            result[s, part] = (h + h * jnp.tanh(h)).astype(BF16)
        rows = pl.ds(step * size, size)
        sent.append(
            pltpu.make_async_copy(result.at[:, rows], out.at[:, 0, rows], sems.at[step])
        )
        sent[-1].start()
    for copy in sent:
        copy.wait()


def convolve(wins, weight, bias, spread):
    whole = pl.BlockSpec(memory_space=pltpu.VMEM)
    return pl.pallas_call(
        conv_kernel,
        out_shape=jax.ShapeDtypeStruct((3, 1, TH * TW, CO), BF16),
        in_specs=[whole] * 7,
        out_specs=pl.BlockSpec(memory_space=pl.ANY),
        scratch_shapes=[
            pltpu.VMEM((9 * WR * WC, 3 * CO), F32),
            pltpu.VMEM((3, TH * TW, CO), BF16),
            pltpu.SemaphoreType.DMA((TH // UROWS,)),
        ],
        compiler_params=pltpu.CompilerParams(vmem_limit_bytes=40 * 2**20),
        name="convolve",
    )(*wins, weight, bias, spread)


def spread_matrix(tile_row, tile_col):
    lane = jnp.arange(DEPTH, dtype=jnp.int32)[None, :]
    pixel = jnp.arange(TH, dtype=jnp.int32)[:, None]
    row_pos = tile_row * TH - 1 + lane // (3 * NEAR * WC) + pixel
    row_node = 4 * tile_row - 1 + pixel // UROWS + (lane // WC) % NEAR
    col_pos = tile_col * TW - 1 + (lane // (NEAR * WC)) % 3 + pixel
    col_node = 6 * tile_col - 1 + lane % WC
    rows = bilinear(row_pos, 2 * BR, FN, row_node)
    cols = bilinear(col_pos, 2 * BC, FN, col_node)
    return (rows[:, None, :] * cols[None, :, :]).astype(BF16).reshape(TH * TW, DEPTH)


def on_device(coarse, region_lat, region_lon, region_order, conv_weight, conv_bias):
    band = lax.axis_index("band")
    own = coarse[0]
    other = lax.ppermute(own, "band", [(i, i ^ 1) for i in range(64)])
    own = with_layout_constraint(own, Layout(major_to_minor=(0, 1, 2)))
    tables, branch = plan(region_lat, region_lon, region_order)
    planes = [[2 * (8 * y + z) + c for z in range(8) for y in range(4)] for c in range(2)]

    def route(capacity):
        def run(own, other, tables):
            cut = pick(capacity, tables, own, other)
            got = lax.all_to_all(cut, "band", 0, 0, axis_index_groups=planes)
            return regroup(capacity, tables, got)

        return run

    tiles = lax.switch(branch[0], [route(cap) for cap in CAPACITIES], own, other, tables)
    band, *tiles = lax.optimization_barrier((band, *tiles))
    wins = [tiles[0]] + [
        lax.ppermute(tiles[hop], "grp", [(i, (i + hop) % 4) for i in range(4)])
        for hop in (2, 1, 3)
    ]
    spread = spread_matrix(band // TCOLS, band % TCOLS)
    weight = jnp.swapaxes(conv_weight, 1, 2)
    return jnp.swapaxes(convolve(wins, weight, conv_bias[None, :], spread), 2, 3)


def solution(mesh):
    in_specs = (P("band", "grp", None, None), P(), P(), P(), P(), P())
    out_specs = P("grp", "band", None, None)
    return jax.shard_map(
        on_device, mesh=mesh, in_specs=in_specs, out_specs=out_specs, check_vma=False
    )
```

```python
import functools

import jax
import jax.numpy as jnp
from jax import lax
from jax.experimental import pallas as pl
from jax.experimental.layout import Layout, with_layout_constraint
from jax.experimental.pallas import tpu as pltpu
from jax.sharding import PartitionSpec as P

CH = 73
CO = 128
FN = 448
BR = 16
BC = 24
CELLS = BR * BC
TCOLS = 8
TH = 56
TW = 56
WR = 6
WC = 8
MAIN = 64
REST = CH - MAIN
ROW = 64
NEAR = 3
DEPTH = 256
UROWS = 14
SPARE = 48
CHIPS = 56
PLACES = 80
HELD = 104
CAPACITIES = (1, 2, 3, 4, 12)
F32 = jnp.float32
BF16 = jnp.bfloat16


def bilinear(positions, node_count, fine_count, nodes):
    coords = (positions.astype(F32) + 0.5) * (node_count / fine_count) - 0.5
    coords = jnp.clip(coords, 0.0, node_count - 1.0)
    weight = jnp.maximum(0.0, 1.0 - jnp.abs(coords - nodes.astype(F32)))
    inside = (positions >= 0) & (positions < fine_count)
    return jnp.where(inside, weight, 0.0)


def plan_kernel(lat, lon, order, held_rows, tables, branch, near_rows, counts, sems):
    fetches = []
    for n, first in enumerate(range(0, CH, 10)):
        part = pl.ds(first, min(10, CH - first))
        fetches.append(
            pltpu.make_async_copy(held_rows.at[part], near_rows.at[part], sems.at[n])
        )
        fetches[-1].start()
    band, group = lax.axis_index("band"), lax.axis_index("grp")
    chip, core = lax.shift_right_logical(band, 1), lax.bitwise_and(band, 1)
    spot = lax.broadcasted_iota(jnp.int32, (8, 128), 1)
    spot_m, spot_g = lax.bitwise_and(spot, 31), lax.shift_right_logical(spot, 5)
    tally = jnp.zeros((8, 128), jnp.int32)
    held = []
    for i in range(12):
        region = order[i]
        lat0, lon0 = lat[region], lon[region]
        lon1 = jnp.where(lon0 == 59, 0, lon0 + 1)
        m0, m1 = lax.shift_right_logical(lat0, 1), lax.shift_right_logical(lat0 + 1, 1)
        g0, g1 = [
            (x >= 15).astype(jnp.int32) + (x >= 30).astype(jnp.int32) + (x >= 45).astype(jnp.int32)
            for x in (lon0, lon1)
        ]
        meets = ((spot_m == m0) | (spot_m == m1)) & ((spot_g == g0) | (spot_g == g1))
        tally = tally + meets.astype(jnp.int32)
        counts[m0] = 0
        counts[m1] = 0
        tables[CHIPS + 2 * i] = m0
        tables[CHIPS + 2 * i + 1] = m1
        held.append((lat0, lon0, lon1, m0, m1, (g0 == group) | (g1 == group)))
    most = jnp.max(tally)
    step = jnp.int32(0)
    for cap in CAPACITIES[:-1]:
        step = step + (most > cap).astype(jnp.int32)
    branch[0] = step
    q = jnp.int32(0)
    for i, (lat0, lon0, lon1, m0, m1, here) in enumerate(held):
        one = here.astype(jnp.int32)
        two = jnp.where(m0 != m1, one, 0)
        n0 = counts[m0]
        counts[m0] = n0 + one
        n1 = counts[m1]
        counts[m1] = n1 + two
        tables[PLACES + 2 * i] = jnp.where(here, n0, -1)
        tables[PLACES + 2 * i + 1] = jnp.where(two == 1, n1, -1)
        mine = here & ((m0 == chip) | (m1 == chip))
        at = jnp.where(mine, 4 * q, SPARE)
        for j in range(2):
            row = lat0 + j - 2 * chip
            side = jnp.where(row == core, 0, 16)
            for k, place in enumerate((lon0, lon1)):
                col = place - 15 * group
                ok = (row >= 0) & (row < 2) & (col >= 0) & (col < 15)
                tables[at + 2 * j + k] = jnp.where(ok, side + col, -1)
        q = q + mine.astype(jnp.int32)
    tables[HELD] = q
    for fetch in fetches:
        fetch.wait()


def plan(lat, lon, order, held_rows):
    smem = pl.BlockSpec(memory_space=pltpu.SMEM)
    return pl.pallas_call(
        plan_kernel,
        out_shape=[jax.ShapeDtypeStruct((n,), jnp.int32) for n in (128, 1)]
        + [pltpu.VMEM(held_rows.shape, held_rows.dtype)],
        in_specs=[smem] * 3 + [pl.BlockSpec(memory_space=pl.ANY)],
        out_specs=[smem] * 2 + [pl.BlockSpec(memory_space=pltpu.VMEM)],
        scratch_shapes=[pltpu.SMEM((33,), jnp.int32), pltpu.SemaphoreType.DMA((8,))],
        name="plan",
    )(lat, lon, order, held_rows)


def payload_rows(capacity):
    return 24 * capacity + 8 * ((capacity + 1) // 2)


def pick_kernel(capacity, tables, own, other, out, window, blocks):
    core = lax.rem(lax.axis_index("band"), 2)
    lane = lax.broadcasted_iota(jnp.int32, (8, 128), 1)
    turn = (
        lax.broadcasted_iota(jnp.int32, (128, 128), 0)
        == lax.broadcasted_iota(jnp.int32, (128, 128), 1)
    ).astype(BF16)
    zeros = jnp.zeros((ROW, 128), F32)
    for n in range(4 * capacity):
        code = jnp.where(n // 4 < tables[HELD], tables[n], -1)

        @pl.when(code < 0)
        def _():
            blocks[n * 128 : (n + 1) * 128] = jnp.zeros((128, CELLS), BF16)

        @pl.when((code >= 0) & (code < 16))
        def _():
            blocks[n * 128 : n * 128 + CH] = own[code]

        @pl.when(code >= 16)
        def _():
            blocks[n * 128 : n * 128 + CH] = other[code - 16]

    for q in range(capacity):
        base = q * 34 * ROW
        window[base : base + ROW] = zeros
        window[base + 33 * ROW : base + 34 * ROW] = zeros
        for r in range(1, 33):
            window[base + r * ROW : base + r * ROW + 8] = zeros[:8]
            window[base + r * ROW + 56 : base + r * ROW + 64] = zeros[:8]
        turned = jnp.concatenate(
            [
                lax.dot_general(
                    turn,
                    blocks[512 * q : 512 * q + 512, 128 * i : 128 * i + 128],
                    (((1,), (1,)), ((), ())),
                    preferred_element_type=F32,
                )
                for i in range(3)
            ],
            axis=0,
        )
        for j in range(2):
            for k in range(2):
                n = 2 * j + k
                for r in range(BR):
                    at = base + (16 * j + r + 1) * ROW + 8 + BC * k
                    window[at : at + BC] = turned[
                        r * BC : (r + 1) * BC, n * 128 : (n + 1) * 128
                    ]

    def emit(a, carry):
        for b in range(4):
            mains, rests = [], []
            for q in range(capacity):
                rows = []
                for i in range(WR):
                    at = q * 34 * ROW + i * ROW + 7 + 12 * b + 6 * core + a * 4 * ROW
                    rows.append(window[pl.ds(at, WC)])
                for i in range(3):
                    mains.append(
                        jnp.where(lane < MAIN, rows[i], pltpu.roll(rows[i + 3], MAIN, 1))
                    )
                side = 64 * (q % 2)
                rest = jnp.zeros((8, 128), F32)
                for i in range(WR):
                    lo = side + REST * i
                    moved = pltpu.roll(rows[i], (lo - MAIN) % 128, 1)
                    rest = jnp.where((lane >= lo) & (lane < lo + REST), moved, rest)
                if q % 2 == 0:
                    rests.append(rest)
                else:
                    rests[-1] = rests[-1] + rest
            out[4 * a + b] = jnp.concatenate(mains + rests, axis=0).astype(BF16)
        return carry

    lax.fori_loop(0, 8, emit, 0, unroll=8 if capacity <= 2 else 1)


def pick(capacity, tables, own, other):
    vmem = pl.BlockSpec(memory_space=pltpu.VMEM)
    smem = pl.BlockSpec(memory_space=pltpu.SMEM)
    return pl.pallas_call(
        functools.partial(pick_kernel, capacity),
        out_shape=jax.ShapeDtypeStruct((32, payload_rows(capacity), 128), BF16),
        in_specs=[smem, vmem, vmem],
        out_specs=vmem,
        scratch_shapes=[
            pltpu.VMEM((capacity * 34 * ROW, 128), F32),
            pltpu.VMEM((capacity * 4 * 128, CELLS), BF16),
        ],
        compiler_params=pltpu.CompilerParams(vmem_limit_bytes=40 * 2**20),
        name="pick",
    )(tables, own, other)


def regroup_kernel(capacity, tables, got, *outs):
    group = lax.axis_index("grp")
    lane = lax.broadcasted_iota(jnp.int32, (8, 128), 1)
    def gather(out, hop, s):
        slot = lax.bitwise_and(group + hop, 3) * 3 + s
        main = jnp.zeros((24, 128), F32)
        rest = jnp.zeros((8, 128), F32)
        for j in range(2):
            place = tables[PLACES + slot * 2 + j]
            part = got[tables[CHIPS + slot * 2 + j]].astype(F32)
            for q in range(capacity):
                here = place == q
                main = main + jnp.where(here, part[24 * q : 24 * q + 24], 0.0)
                at = 24 * capacity + 8 * (q // 2)
                side = part[at : at + 8]
                if q % 2:
                    side = pltpu.roll(side, 64, 1)
                rest = rest + jnp.where(here, side, 0.0)
        rows = []
        for i in range(WR):
            body = main[8 * (i % 3) : 8 * (i % 3) + 8]
            if i >= 3:
                body = pltpu.roll(body, 64, 1)
            tail = pltpu.roll(rest, (MAIN - REST * i) % 128, 1)
            row = jnp.where(lane < MAIN, body, jnp.where(lane < CH, tail, 0.0))
            rows.append(row)
        out[WR * WC * s : WR * WC * (s + 1)] = jnp.concatenate(rows, axis=0).astype(BF16)

    for hop in range(4):
        for s in range(3):
            gather(outs[hop], hop, s)


def regroup(capacity, tables, got):
    vmem = pl.BlockSpec(memory_space=pltpu.VMEM)
    smem = pl.BlockSpec(memory_space=pltpu.SMEM)
    return pl.pallas_call(
        functools.partial(regroup_kernel, capacity),
        out_shape=[jax.ShapeDtypeStruct((3 * WR * WC, 128), BF16)] * 4,
        in_specs=[smem, vmem],
        out_specs=[vmem] * 4,
        compiler_params=pltpu.CompilerParams(vmem_limit_bytes=24 * 2**20),
        name="regroup",
    )(tables, got)


def conv_kernel(win0, win1, win2, win3, weight, bias, spread, out, taps, result, sems):
    n = WR * WC
    cells = win0[...].astype(F32) + win1[...].astype(F32)
    cells = cells + (win2[...].astype(F32) + win3[...].astype(F32))
    cells = cells.astype(BF16)[:, :CH]
    every = jnp.concatenate([weight[t] for t in range(9)], axis=1)
    made = jnp.dot(cells, every, preferred_element_type=F32) * 0.5
    for t in range(9):
        for s in range(3):
            taps[t * n : (t + 1) * n, s * CO : (s + 1) * CO] = made[
                s * n : (s + 1) * n, t * CO : (t + 1) * CO
            ]
    half_bias = 0.5 * bias[...]
    size = UROWS * TW
    sent = []
    for step in range(TH // UROWS):
        near = [
            taps[t * n + WC * step : t * n + WC * (step + NEAR)] for t in range(9)
        ]
        near.append(jnp.zeros((DEPTH - 9 * NEAR * WC, 3 * CO), F32))
        near = jnp.concatenate(near, axis=0).astype(BF16)
        part = slice(step * size, (step + 1) * size)
        half = jnp.dot(spread[part], near, preferred_element_type=F32)
        for s in range(3):
            h = half[:, s * CO : (s + 1) * CO] + half_bias
            result[s, part] = (h + h * jnp.tanh(h)).astype(BF16)
        rows = pl.ds(step * size, size)
        sent.append(
            pltpu.make_async_copy(result.at[:, rows], out.at[:, 0, rows], sems.at[step])
        )
        sent[-1].start()
    for copy in sent:
        copy.wait()


def convolve(wins, weight, bias, spread):
    whole = pl.BlockSpec(memory_space=pltpu.VMEM)
    return pl.pallas_call(
        conv_kernel,
        out_shape=jax.ShapeDtypeStruct((3, 1, TH * TW, CO), BF16),
        in_specs=[whole] * 7,
        out_specs=pl.BlockSpec(memory_space=pl.ANY),
        scratch_shapes=[
            pltpu.VMEM((9 * WR * WC, 3 * CO), F32),
            pltpu.VMEM((3, TH * TW, CO), BF16),
            pltpu.SemaphoreType.DMA((TH // UROWS,)),
        ],
        compiler_params=pltpu.CompilerParams(vmem_limit_bytes=40 * 2**20),
        name="convolve",
    )(*wins, weight, bias, spread)


def spread_matrix(tile_row, tile_col):
    lane = jnp.arange(DEPTH, dtype=jnp.int32)[None, :]
    pixel = jnp.arange(TH, dtype=jnp.int32)[:, None]
    row_pos = tile_row * TH - 1 + lane // (3 * NEAR * WC) + pixel
    row_node = 4 * tile_row - 1 + pixel // UROWS + (lane // WC) % NEAR
    col_pos = tile_col * TW - 1 + (lane // (NEAR * WC)) % 3 + pixel
    col_node = 6 * tile_col - 1 + lane % WC
    rows = bilinear(row_pos, 2 * BR, FN, row_node)
    cols = bilinear(col_pos, 2 * BC, FN, col_node)
    return (rows[:, None, :] * cols[None, :, :]).astype(BF16).reshape(TH * TW, DEPTH)


def on_device(coarse, region_lat, region_lon, region_order, conv_weight, conv_bias):
    band = lax.axis_index("band")
    own = coarse[0]
    other = lax.ppermute(own, "band", [(i, i ^ 1) for i in range(64)])
    tables, branch, own = plan(
        region_lat, region_lon, region_order, jnp.swapaxes(own, 0, 1)
    )
    own = with_layout_constraint(jnp.swapaxes(own, 0, 1), Layout(major_to_minor=(0, 1, 2)))
    planes = [[2 * m + c for m in range(32)] for c in range(2)]

    def route(capacity):
        def run(own, other, tables):
            cut = pick(capacity, tables, own, other)
            got = lax.all_to_all(cut, "band", 0, 0, axis_index_groups=planes)
            return regroup(capacity, tables, got)

        return run

    tiles = lax.switch(branch[0], [route(cap) for cap in CAPACITIES], own, other, tables)
    band, *tiles = lax.optimization_barrier((band, *tiles))
    wins = [tiles[0]] + [
        lax.ppermute(tiles[hop], "grp", [(i, (i + hop) % 4) for i in range(4)])
        for hop in (2, 1, 3)
    ]
    spread = spread_matrix(band // TCOLS, band % TCOLS)
    weight = jnp.swapaxes(conv_weight, 1, 2)
    return jnp.swapaxes(convolve(wins, weight, conv_bias[None, :], spread), 2, 3)


def solution(mesh):
    in_specs = (P("band", "grp", None, None), P(), P(), P(), P(), P())
    out_specs = P("grp", "band", None, None)
    return jax.shard_map(
        on_device, mesh=mesh, in_specs=in_specs, out_specs=out_specs, check_vma=False
    )
```

```python
import functools

import jax
import jax.numpy as jnp
from jax import lax
from jax.experimental import pallas as pl
from jax.experimental.layout import Layout, with_layout_constraint
from jax.experimental.pallas import tpu as pltpu
from jax.sharding import PartitionSpec as P

CH = 73
CO = 128
FN = 448
BR = 16
BC = 24
CELLS = BR * BC
TCOLS = 8
TH = 56
TW = 56
WR = 6
WC = 8
MAIN = 64
REST = CH - MAIN
ROW = 64
NEAR = 3
DEPTH = 256
UROWS = 14
SPARE = 48
CHIPS = 56
PLACES = 80
HELD = 104
CAPACITIES = (1, 2, 3, 4, 12)
F32 = jnp.float32
BF16 = jnp.bfloat16


def bilinear(positions, node_count, fine_count, nodes):
    coords = (positions.astype(F32) + 0.5) * (node_count / fine_count) - 0.5
    coords = jnp.clip(coords, 0.0, node_count - 1.0)
    weight = jnp.maximum(0.0, 1.0 - jnp.abs(coords - nodes.astype(F32)))
    inside = (positions >= 0) & (positions < fine_count)
    return jnp.where(inside, weight, 0.0)


def rank_of(chip):
    return lax.bitwise_and(chip, 7) * 4 + lax.shift_right_logical(chip, 3)


def plan_kernel(lat, lon, order, held_rows, tables, branch, near_rows, counts, sems):
    fetches = []
    for n, first in enumerate(range(0, CH, 10)):
        part = pl.ds(first, min(10, CH - first))
        fetches.append(
            pltpu.make_async_copy(held_rows.at[part], near_rows.at[part], sems.at[n])
        )
        fetches[-1].start()
    band, group = lax.axis_index("band"), lax.axis_index("grp")
    chip, core = lax.shift_right_logical(band, 1), lax.bitwise_and(band, 1)
    spot = lax.broadcasted_iota(jnp.int32, (8, 128), 1)
    spot_m, spot_g = lax.bitwise_and(spot, 31), lax.shift_right_logical(spot, 5)
    tally = jnp.zeros((8, 128), jnp.int32)
    held = []
    for i in range(12):
        region = order[i]
        lat0, lon0 = lat[region], lon[region]
        lon1 = jnp.where(lon0 == 59, 0, lon0 + 1)
        m0, m1 = lax.shift_right_logical(lat0, 1), lax.shift_right_logical(lat0 + 1, 1)
        g0, g1 = [
            (x >= 15).astype(jnp.int32) + (x >= 30).astype(jnp.int32) + (x >= 45).astype(jnp.int32)
            for x in (lon0, lon1)
        ]
        meets = ((spot_m == m0) | (spot_m == m1)) & ((spot_g == g0) | (spot_g == g1))
        tally = tally + meets.astype(jnp.int32)
        counts[m0] = 0
        counts[m1] = 0
        tables[CHIPS + 2 * i] = rank_of(m0)
        tables[CHIPS + 2 * i + 1] = rank_of(m1)
        held.append((lat0, lon0, lon1, m0, m1, (g0 == group) | (g1 == group)))
    most = jnp.max(tally)
    step = jnp.int32(0)
    for cap in CAPACITIES[:-1]:
        step = step + (most > cap).astype(jnp.int32)
    branch[0] = step
    q = jnp.int32(0)
    for i, (lat0, lon0, lon1, m0, m1, here) in enumerate(held):
        one = here.astype(jnp.int32)
        two = jnp.where(m0 != m1, one, 0)
        n0 = counts[m0]
        counts[m0] = n0 + one
        n1 = counts[m1]
        counts[m1] = n1 + two
        tables[PLACES + 2 * i] = jnp.where(here, n0, -1)
        tables[PLACES + 2 * i + 1] = jnp.where(two == 1, n1, -1)
        mine = here & ((m0 == chip) | (m1 == chip))
        at = jnp.where(mine, 4 * q, SPARE)
        for j in range(2):
            row = lat0 + j - 2 * chip
            side = jnp.where(row == core, 0, 16)
            for k, place in enumerate((lon0, lon1)):
                col = place - 15 * group
                ok = (row >= 0) & (row < 2) & (col >= 0) & (col < 15)
                tables[at + 2 * j + k] = jnp.where(ok, side + col, -1)
        q = q + mine.astype(jnp.int32)
    tables[HELD] = q
    for fetch in fetches:
        fetch.wait()


def plan(lat, lon, order, held_rows):
    smem = pl.BlockSpec(memory_space=pltpu.SMEM)
    return pl.pallas_call(
        plan_kernel,
        out_shape=[jax.ShapeDtypeStruct((n,), jnp.int32) for n in (128, 1)]
        + [pltpu.VMEM(held_rows.shape, held_rows.dtype)],
        in_specs=[smem] * 3 + [pl.BlockSpec(memory_space=pl.ANY)],
        out_specs=[smem] * 2 + [pl.BlockSpec(memory_space=pltpu.VMEM)],
        scratch_shapes=[pltpu.SMEM((33,), jnp.int32), pltpu.SemaphoreType.DMA((8,))],
        name="plan",
    )(lat, lon, order, held_rows)


def payload_rows(capacity):
    return 24 * capacity + 8 * ((capacity + 1) // 2)


def pick_kernel(capacity, tables, own, other, out, window, blocks):
    core = lax.rem(lax.axis_index("band"), 2)
    lane = lax.broadcasted_iota(jnp.int32, (8, 128), 1)
    turn = (
        lax.broadcasted_iota(jnp.int32, (128, 128), 0)
        == lax.broadcasted_iota(jnp.int32, (128, 128), 1)
    ).astype(BF16)
    zeros = jnp.zeros((ROW, 128), F32)
    for n in range(4 * capacity):
        code = jnp.where(n // 4 < tables[HELD], tables[n], -1)

        @pl.when(code < 0)
        def _():
            blocks[n * 128 : (n + 1) * 128] = jnp.zeros((128, CELLS), BF16)

        @pl.when((code >= 0) & (code < 16))
        def _():
            blocks[n * 128 : n * 128 + CH] = own[code]

        @pl.when(code >= 16)
        def _():
            blocks[n * 128 : n * 128 + CH] = other[code - 16]

    for q in range(capacity):
        base = q * 34 * ROW
        window[base : base + ROW] = zeros
        window[base + 33 * ROW : base + 34 * ROW] = zeros
        for r in range(1, 33):
            window[base + r * ROW : base + r * ROW + 8] = zeros[:8]
            window[base + r * ROW + 56 : base + r * ROW + 64] = zeros[:8]
        turned = jnp.concatenate(
            [
                lax.dot_general(
                    turn,
                    blocks[512 * q : 512 * q + 512, 128 * i : 128 * i + 128],
                    (((1,), (1,)), ((), ())),
                    preferred_element_type=F32,
                )
                for i in range(3)
            ],
            axis=0,
        )
        for j in range(2):
            for k in range(2):
                n = 2 * j + k
                for r in range(BR):
                    at = base + (16 * j + r + 1) * ROW + 8 + BC * k
                    window[at : at + BC] = turned[
                        r * BC : (r + 1) * BC, n * 128 : (n + 1) * 128
                    ]

    def emit(a, carry):
        for b in range(4):
            mains, rests = [], []
            for q in range(capacity):
                rows = []
                for i in range(WR):
                    at = q * 34 * ROW + i * ROW + 7 + 12 * b + 6 * core + a * 4 * ROW
                    rows.append(window[pl.ds(at, WC)])
                for i in range(3):
                    mains.append(
                        jnp.where(lane < MAIN, rows[i], pltpu.roll(rows[i + 3], MAIN, 1))
                    )
                side = 64 * (q % 2)
                rest = jnp.zeros((8, 128), F32)
                for i in range(WR):
                    lo = side + REST * i
                    moved = pltpu.roll(rows[i], (lo - MAIN) % 128, 1)
                    rest = jnp.where((lane >= lo) & (lane < lo + REST), moved, rest)
                if q % 2 == 0:
                    rests.append(rest)
                else:
                    rests[-1] = rests[-1] + rest
            chip = 4 * a + b
            out[rank_of(chip)] = jnp.concatenate(mains + rests, axis=0).astype(BF16)
        return carry

    lax.fori_loop(0, 8, emit, 0, unroll=8 if capacity <= 2 else 1)


def pick(capacity, tables, own, other):
    vmem = pl.BlockSpec(memory_space=pltpu.VMEM)
    smem = pl.BlockSpec(memory_space=pltpu.SMEM)
    return pl.pallas_call(
        functools.partial(pick_kernel, capacity),
        out_shape=jax.ShapeDtypeStruct((32, payload_rows(capacity), 128), BF16),
        in_specs=[smem, vmem, vmem],
        out_specs=vmem,
        scratch_shapes=[
            pltpu.VMEM((capacity * 34 * ROW, 128), F32),
            pltpu.VMEM((capacity * 4 * 128, CELLS), BF16),
        ],
        compiler_params=pltpu.CompilerParams(vmem_limit_bytes=40 * 2**20),
        name="pick",
    )(tables, own, other)


def regroup_kernel(capacity, tables, got, *outs):
    group = lax.axis_index("grp")
    lane = lax.broadcasted_iota(jnp.int32, (8, 128), 1)
    def gather(out, hop, s):
        slot = lax.bitwise_and(group + hop, 3) * 3 + s
        main = jnp.zeros((24, 128), F32)
        rest = jnp.zeros((8, 128), F32)
        for j in range(2):
            place = tables[PLACES + slot * 2 + j]
            part = got[tables[CHIPS + slot * 2 + j]].astype(F32)
            for q in range(capacity):
                here = place == q
                main = main + jnp.where(here, part[24 * q : 24 * q + 24], 0.0)
                at = 24 * capacity + 8 * (q // 2)
                side = part[at : at + 8]
                if q % 2:
                    side = pltpu.roll(side, 64, 1)
                rest = rest + jnp.where(here, side, 0.0)
        rows = []
        for i in range(WR):
            body = main[8 * (i % 3) : 8 * (i % 3) + 8]
            if i >= 3:
                body = pltpu.roll(body, 64, 1)
            tail = pltpu.roll(rest, (MAIN - REST * i) % 128, 1)
            row = jnp.where(lane < MAIN, body, jnp.where(lane < CH, tail, 0.0))
            rows.append(row)
        out[WR * WC * s : WR * WC * (s + 1)] = jnp.concatenate(rows, axis=0).astype(BF16)

    for hop in range(4):
        for s in range(3):
            gather(outs[hop], hop, s)


def regroup(capacity, tables, got):
    vmem = pl.BlockSpec(memory_space=pltpu.VMEM)
    smem = pl.BlockSpec(memory_space=pltpu.SMEM)
    return pl.pallas_call(
        functools.partial(regroup_kernel, capacity),
        out_shape=[jax.ShapeDtypeStruct((3 * WR * WC, 128), BF16)] * 4,
        in_specs=[smem, vmem],
        out_specs=[vmem] * 4,
        compiler_params=pltpu.CompilerParams(vmem_limit_bytes=24 * 2**20),
        name="regroup",
    )(tables, got)


def conv_kernel(win0, win1, win2, win3, weight, bias, spread, out, taps, result, sems):
    n = WR * WC
    cells = win0[...].astype(F32) + win1[...].astype(F32)
    cells = cells + (win2[...].astype(F32) + win3[...].astype(F32))
    cells = cells.astype(BF16)[:, :CH]
    every = jnp.concatenate([weight[t] for t in range(9)], axis=1)
    made = jnp.dot(cells, every, preferred_element_type=F32) * 0.5
    for t in range(9):
        for s in range(3):
            taps[t * n : (t + 1) * n, s * CO : (s + 1) * CO] = made[
                s * n : (s + 1) * n, t * CO : (t + 1) * CO
            ]
    half_bias = 0.5 * bias[...]
    size = UROWS * TW
    sent = []
    for step in range(TH // UROWS):
        near = [
            taps[t * n + WC * step : t * n + WC * (step + NEAR)] for t in range(9)
        ]
        near.append(jnp.zeros((DEPTH - 9 * NEAR * WC, 3 * CO), F32))
        near = jnp.concatenate(near, axis=0).astype(BF16)
        part = slice(step * size, (step + 1) * size)
        half = jnp.dot(spread[part], near, preferred_element_type=F32)
        for s in range(3):
            h = half[:, s * CO : (s + 1) * CO] + half_bias
            result[s, part] = (h + h * jnp.tanh(h)).astype(BF16)
        rows = pl.ds(step * size, size)
        sent.append(
            pltpu.make_async_copy(result.at[:, rows], out.at[:, 0, rows], sems.at[step])
        )
        sent[-1].start()
    for copy in sent:
        copy.wait()


def convolve(wins, weight, bias, spread):
    whole = pl.BlockSpec(memory_space=pltpu.VMEM)
    return pl.pallas_call(
        conv_kernel,
        out_shape=jax.ShapeDtypeStruct((3, 1, TH * TW, CO), BF16),
        in_specs=[whole] * 7,
        out_specs=pl.BlockSpec(memory_space=pl.ANY),
        scratch_shapes=[
            pltpu.VMEM((9 * WR * WC, 3 * CO), F32),
            pltpu.VMEM((3, TH * TW, CO), BF16),
            pltpu.SemaphoreType.DMA((TH // UROWS,)),
        ],
        compiler_params=pltpu.CompilerParams(vmem_limit_bytes=40 * 2**20),
        name="convolve",
    )(*wins, weight, bias, spread)


def spread_matrix(tile_row, tile_col):
    lane = jnp.arange(DEPTH, dtype=jnp.int32)[None, :]
    pixel = jnp.arange(TH, dtype=jnp.int32)[:, None]
    row_pos = tile_row * TH - 1 + lane // (3 * NEAR * WC) + pixel
    row_node = 4 * tile_row - 1 + pixel // UROWS + (lane // WC) % NEAR
    col_pos = tile_col * TW - 1 + (lane // (NEAR * WC)) % 3 + pixel
    col_node = 6 * tile_col - 1 + lane % WC
    rows = bilinear(row_pos, 2 * BR, FN, row_node)
    cols = bilinear(col_pos, 2 * BC, FN, col_node)
    return (rows[:, None, :] * cols[None, :, :]).astype(BF16).reshape(TH * TW, DEPTH)


def on_device(coarse, region_lat, region_lon, region_order, conv_weight, conv_bias):
    band = lax.axis_index("band")
    own = coarse[0]
    other = lax.ppermute(own, "band", [(i, i ^ 1) for i in range(64)])
    tables, branch, own = plan(
        region_lat, region_lon, region_order, jnp.swapaxes(own, 0, 1)
    )
    own = with_layout_constraint(jnp.swapaxes(own, 0, 1), Layout(major_to_minor=(0, 1, 2)))
    planes = [[2 * (8 * y + z) + c for z in range(8) for y in range(4)] for c in range(2)]

    def route(capacity):
        def run(own, other, tables):
            cut = pick(capacity, tables, own, other)
            got = lax.all_to_all(cut, "band", 0, 0, axis_index_groups=planes)
            return regroup(capacity, tables, got)

        return run

    tiles = lax.switch(branch[0], [route(cap) for cap in CAPACITIES], own, other, tables)
    band, *tiles = lax.optimization_barrier((band, *tiles))
    wins = [tiles[0]] + [
        lax.ppermute(tiles[hop], "grp", [(i, (i + hop) % 4) for i in range(4)])
        for hop in (2, 1, 3)
    ]
    spread = spread_matrix(band // TCOLS, band % TCOLS)
    weight = jnp.swapaxes(conv_weight, 1, 2)
    return jnp.swapaxes(convolve(wins, weight, conv_bias[None, :], spread), 2, 3)


def solution(mesh):
    in_specs = (P("band", "grp", None, None), P(), P(), P(), P(), P())
    out_specs = P("grp", "band", None, None)
    return jax.shard_map(
        on_device, mesh=mesh, in_specs=in_specs, out_specs=out_specs, check_vma=False
    )
```
